32 devices in a mesh: section: 4 (over x, core), dp: 8 (over z, y).
Axes of the slice: x: 2, y: 2, z: 4, core: 2. Of those that a mesh axis runs over, the one named last changes fastest.
Arguments:
- inputs: bfloat16 [2, 1024, 1536], P(None, 'dp'), may hold values from -6 to 6
- grad_out: bfloat16 [2, 1024, 1536], P(None, 'dp'), may hold values from -6 to 6
- w_conv: bfloat16 [4, 4608, 768], P('section'), may hold values from -0.09375 to 0.09375
- w_point: bfloat16 [4, 768, 1536], P('section'), may hold values from -0.21875 to 0.21875
- gain_conv: float32 [4, 1536], P('section'), may hold values from 0.25 to 1.75
- gain_point: float32 [4, 768], P('section'), may hold values from 0.25 to 1.75
Outputs:
- grad_w_conv: float32 [4, 4608, 768], P('section', 'dp')
- grad_w_point: float32 [4, 768, 1536], P('section', 'dp')
- grad_gain_conv: float32 [4, 1536], P('section', 'dp')
- grad_gain_point: float32 [4, 768], P('section', 'dp')
- grad_acts: bfloat16 [4, 2, 1024, 1536], P('section', None, 'dp')
The draws below stay inside these ranges and needn't reach their ends.
All inputs are finite; a program needn't handle non-finite values.
Results may differ from the reference program's by a relative error of at most 0.034.
Values may be sent and summed in bfloat16 or wider, within the bound.
A program may use at most 128 MiB of HBM per device.

```python
import math
import jax
import jax.numpy as jnp
from jax import lax

C = 1536
M = 768
MB = 2
SECTIONS = 4
LEN = 1024
N_SECTION = 4


def block_levels(stream_key, dims, shards, least, high):
    level, own = 1.0, jax.random.fold_in(stream_key, 6)
    for dim, shards_of in shards:
        steps = jnp.exp(jax.random.uniform(jax.random.fold_in(own, dim), (shards_of,), jnp.float32, least / len(shards), high / len(shards)))
        level = level * jnp.repeat(steps, dims[dim] // shards_of).reshape([-1 if axis == dim else 1 for axis in range(len(dims))])
    return level


def noise(stream_key, extent, scale, most, cuts=(), held_as=jnp.bfloat16):
    entries = scale * jax.random.normal(stream_key, extent, jnp.float32)
    if cuts:
        entries = entries * block_levels(stream_key, extent, cuts, -0.22, 0.18)
    return jnp.clip(entries, -most, most).astype(held_as)


def setup_inputs(seed: int = 0) -> dict:
    key_list = jax.random.split(jax.random.key(seed), 7)
    inputs = noise(key_list[0], (MB, LEN, C), 1.0, 6.0, ((1, 8),))
    grad_out = noise(key_list[1], (MB, LEN, C), 1.0, 6.0, ((1, 8),))
    w_conv = noise(key_list[2], (SECTIONS, 3 * C, M), (3 * C) ** -0.5, 0.09375, ((0, 4),))
    w_point = noise(key_list[3], (SECTIONS, M, C), M ** -0.5, 0.21875, ((0, 4),))
    gain_conv = jnp.clip(1.0 + 0.15 * jax.random.normal(key_list[4], (SECTIONS, C), jnp.float32), 0.25, 1.75)
    gain_point = jnp.clip(1.0 + 0.15 * jax.random.normal(key_list[5], (SECTIONS, M), jnp.float32), 0.25, 1.75)
    return dict(inputs=inputs, grad_out=grad_out, w_conv=w_conv, w_point=w_point, gain_conv=gain_conv, gain_point=gain_point)


EPSILON = 1e-06

def norm_act(values, scales):
    mean_sq = lax.optimization_barrier(jnp.mean(values * values, axis=-1, keepdims=True))
    return jax.nn.gelu(values * lax.rsqrt(mean_sq + EPSILON) * scales)

def shifted(values, dilation, offset):
    margin_rows = values.shape[1] // 2
    padded = jnp.pad(values, ((0, 0), (margin_rows, margin_rows), (0, 0)))
    return lax.dynamic_slice_in_dim(padded, margin_rows + offset * dilation, values.shape[1], 1)

def unfold(activations, dilation):
    joined = jnp.concatenate([shifted(activations, dilation, -1), activations, shifted(activations, dilation, 1)], axis=-1)
    return joined.reshape(-1, joined.shape[-1])

def block_forward(incoming, weight_conv, weight_point, scale_conv, scale_point, dilation):
    batches, positions, channels = incoming.shape
    widened = incoming.astype(jnp.float32)
    activations = norm_act(widened, scale_conv).astype(jnp.bfloat16)
    columns = unfold(activations, dilation)
    conv_out = jnp.dot(columns, weight_conv, preferred_element_type=jnp.float32)
    mixture = norm_act(conv_out, scale_point).astype(jnp.bfloat16)
    branch = jnp.dot(mixture, weight_point, preferred_element_type=jnp.float32)
    outputs = (widened.reshape(-1, channels) + branch).astype(jnp.bfloat16)
    return (outputs.reshape(batches, positions, channels), conv_out)

def block_backward(incoming, conv_out, upstream, weight_conv, weight_point, scale_conv, scale_point, dilation):
    batches, positions, channels = incoming.shape
    widened = incoming.astype(jnp.float32)
    acts_wide, pull_conv = jax.vjp(norm_act, widened, scale_conv)
    activations = acts_wide.astype(jnp.bfloat16)
    columns = unfold(activations, dilation)
    mix_wide, pull_point = jax.vjp(norm_act, conv_out, scale_point)
    mixture = mix_wide.astype(jnp.bfloat16)
    flat_up = upstream.reshape(-1, channels)
    grad_point = jnp.dot(mixture.T, flat_up, preferred_element_type=jnp.float32)
    grad_mixture = jnp.dot(flat_up, weight_point.T, preferred_element_type=jnp.float32)
    grad_conv_wide, grad_scale_point = pull_point(grad_mixture)
    grad_conv = grad_conv_wide.astype(jnp.bfloat16)
    grad_wconv = jnp.dot(columns.T, grad_conv, preferred_element_type=jnp.float32)
    grad_cols = jnp.dot(grad_conv, weight_conv.T, preferred_element_type=jnp.float32)
    grad_cols = grad_cols.reshape(batches, positions, 3 * channels)
    grad_acts = shifted(grad_cols[:, :, :channels], dilation, 1)
    grad_acts = grad_acts + grad_cols[:, :, channels:2 * channels]
    grad_acts = grad_acts + shifted(grad_cols[:, :, 2 * channels:], dilation, -1)
    grad_widened, grad_scale_conv = pull_conv(grad_acts)
    downstream = (upstream.astype(jnp.float32) + grad_widened).astype(jnp.bfloat16)
    return (downstream, grad_wconv, grad_point, grad_scale_conv, grad_scale_point)

def reference(inputs, grad_out, w_conv, w_point, gain_conv, gain_point):
    stored = []
    stored_conv = []
    current = inputs
    for layer_index in range(N_SECTION):
        dilation = 3 ** layer_index // 2 ** layer_index
        stored.append(current)
        current, conv_out = block_forward(current, w_conv[layer_index], w_point[layer_index], gain_conv[layer_index], gain_point[layer_index], dilation)
        stored_conv.append(conv_out)
    upstream = grad_out
    conv_grads = [None] * N_SECTION
    point_grads = [None] * N_SECTION
    gconv_grads = [None] * N_SECTION
    gpoint_grads = [None] * N_SECTION
    input_grads = [None] * N_SECTION
    for layer_index in reversed(range(N_SECTION)):
        dilation = 3 ** layer_index // 2 ** layer_index
        upstream, grad_wconv, grad_point, grad_sc, grad_sp = block_backward(stored[layer_index], stored_conv[layer_index], upstream, w_conv[layer_index], w_point[layer_index], gain_conv[layer_index], gain_point[layer_index], dilation)
        conv_grads[layer_index] = grad_wconv
        point_grads[layer_index] = grad_point
        gconv_grads[layer_index] = grad_sc
        gpoint_grads[layer_index] = grad_sp
        input_grads[layer_index] = upstream
    norm_scale = 1.0 / math.sqrt(inputs.shape[0] * inputs.shape[1])
    return (jnp.stack(conv_grads) * norm_scale, jnp.stack(point_grads) * norm_scale, jnp.stack(gconv_grads) * norm_scale, jnp.stack(gpoint_grads) * norm_scale, jnp.stack(input_grads))
```

```python
import math

import jax
import jax.numpy as jnp
from jax import lax
from jax.sharding import PartitionSpec as P

EPSILON = 1e-06


def with_halo(cells, sides, width):
    for axis, dim in sides:
        count = lax.axis_size(axis)
        ends = count - 1
        head = lax.slice_in_dim(cells, 0, width, axis=dim)
        tail = lax.slice_in_dim(cells, cells.shape[dim] - width, cells.shape[dim], axis=dim)
        cells = jnp.concatenate(
            [
                lax.ppermute(tail, axis, [(i, (i + 1) % count) for i in range(ends)]),
                cells,
                lax.ppermute(head, axis, [((i + 1) % count, i) for i in range(ends)]),
            ],
            axis=dim,
        )
    return cells


def shifted(shard, axis, by):
    devices = lax.axis_size(axis)
    pairs = [(i, i + by) for i in range(devices) if 0 <= i + by < devices]
    return lax.ppermute(shard, axis, pairs)


def norm_act(values, scales):
    mean_sq = jnp.mean(values * values, axis=-1, keepdims=True)
    return jax.nn.gelu(values * lax.rsqrt(mean_sq + EPSILON) * scales)


def tap_columns(padded, dilation, reach, positions):
    earlier = lax.dynamic_slice_in_dim(padded, reach - dilation, positions, 0)
    central = lax.dynamic_slice_in_dim(padded, reach, positions, 0)
    later_rows = lax.dynamic_slice_in_dim(padded, reach + dilation, positions, 0)
    return jnp.concatenate([earlier, central, later_rows], axis=-1)


def contract_rows(left, right):
    return lax.dot_general(
        left, right, (((0,), (0,)), ((), ())), preferred_element_type=jnp.float32
    )


def times_transposed(left, right):
    return lax.dot_general(
        left, right, (((1,), (1,)), ((), ())), preferred_element_type=jnp.float32
    )


def on_device(inputs, grad_out, w_conv, w_point, gain_conv, gain_point):
    micro_count, positions, channels = inputs.shape
    section_index = lax.axis_index("section")
    section_count = lax.axis_size("section")
    group_size = lax.axis_size("dp")
    norm_scale = 1.0 / math.sqrt(micro_count * positions * group_size)
    reach = 3 ** (section_count - 1) // 2 ** (section_count - 1)
    dilation_table = jnp.array(
        [3**depth_index // 2**depth_index for depth_index in range(section_count)], jnp.int32
    )
    dilation = dilation_table[section_index]
    weight_conv = w_conv[0]
    weight_point = w_point[0]
    scale_conv = gain_conv[0]
    scale_point = gain_point[0]
    inner = weight_conv.shape[1]
    tap_weights = weight_conv.reshape(3, channels, inner)
    tick_total = section_count + micro_count - 1
    zero_rows = jnp.zeros((positions, channels), jnp.bfloat16)

    def place(store, value, slot, active):
        old = lax.dynamic_index_in_dim(store, slot, 0, keepdims=False)
        return lax.dynamic_update_index_in_dim(store, jnp.where(active, value, old), slot, 0)

    received = zero_rows
    stored = jnp.zeros_like(inputs)
    column_store = jnp.zeros((micro_count, positions, 3 * channels), jnp.bfloat16)
    mix_store = jnp.zeros((micro_count, positions, inner), jnp.bfloat16)
    conv_store = jnp.zeros((micro_count, positions, inner), jnp.float32)
    for tick in range(tick_total):
        micro_step = tick - section_index
        active = (micro_step >= 0) & (micro_step < micro_count)
        slot = jnp.clip(micro_step, 0, micro_count - 1)
        own_rows = lax.dynamic_index_in_dim(inputs, slot, 0, keepdims=False)
        incoming = jnp.where(section_index == 0, own_rows, received)
        widened = incoming.astype(jnp.float32)
        activations = norm_act(widened, scale_conv).astype(jnp.bfloat16)
        padded = with_halo(activations, (("dp", 0),), reach)
        columns = tap_columns(padded, dilation, reach, positions)
        conv_out = jnp.dot(columns, weight_conv, preferred_element_type=jnp.float32)
        mixture = norm_act(conv_out, scale_point).astype(jnp.bfloat16)
        stored = place(stored, incoming, slot, active)
        column_store = place(column_store, columns, slot, active)
        mix_store = place(mix_store, mixture, slot, active)
        conv_store = place(conv_store, conv_out, slot, active)
        if tick < tick_total - 1:
            branch = jnp.dot(mixture, weight_point, preferred_element_type=jnp.float32)
            received = shifted((widened + branch).astype(jnp.bfloat16), "section", 1)

    dp_index = lax.axis_index("dp")
    own_columns = lax.all_to_all(
        column_store.reshape(micro_count * positions, group_size, 3 * channels // group_size),
        "dp", 1, 0, tiled=False,
    )
    rows = micro_count * positions * group_size
    own_mix = lax.all_to_all(
        mix_store.reshape(micro_count * positions, group_size, inner // group_size),
        "dp", 1, 0, tiled=False,
    )

    received = zero_rows
    input_grads = jnp.zeros_like(inputs)
    up_store = jnp.zeros_like(inputs)
    q_store = jnp.zeros((micro_count, positions, inner), jnp.bfloat16)
    gain_c = jnp.zeros((channels,), jnp.float32)
    gain_p = jnp.zeros((inner,), jnp.float32)
    for tick in range(tick_total):
        micro_step = tick - (section_count - 1 - section_index)
        active = (micro_step >= 0) & (micro_step < micro_count)
        slot = jnp.clip(micro_step, 0, micro_count - 1)
        own_rows = lax.dynamic_index_in_dim(grad_out, slot, 0, keepdims=False)
        upstream = jnp.where(section_index == section_count - 1, own_rows, received)
        saved_rows = lax.dynamic_index_in_dim(stored, slot, 0, keepdims=False)
        conv_out = lax.dynamic_index_in_dim(conv_store, slot, 0, keepdims=False)
        grad_mixture = times_transposed(upstream, weight_point)
        unused_mix, pull_point = jax.vjp(norm_act, conv_out, scale_point)
        grad_conv_wide, grad_sp = pull_point(grad_mixture)
        grad_conv = grad_conv_wide.astype(jnp.bfloat16)
        grad_pad = with_halo(grad_conv, (("dp", 0),), reach)
        ahead_rows = lax.dynamic_slice_in_dim(grad_pad, reach + dilation, positions, 0)
        behind = lax.dynamic_slice_in_dim(grad_pad, reach - dilation, positions, 0)
        grad_acts = times_transposed(ahead_rows, tap_weights[0]) + times_transposed(
            grad_conv, tap_weights[1]
        )
        grad_acts = grad_acts + times_transposed(behind, tap_weights[2])
        widened = saved_rows.astype(jnp.float32)
        unused_acts, pull_conv = jax.vjp(norm_act, widened, scale_conv)
        grad_widened, grad_sc = pull_conv(grad_acts)
        downstream = (upstream.astype(jnp.float32) + grad_widened).astype(jnp.bfloat16)
        gain_c = gain_c + jnp.where(active, grad_sc, 0.0)
        gain_p = gain_p + jnp.where(active, grad_sp, 0.0)
        up_store = place(up_store, upstream, slot, active)
        q_store = place(q_store, grad_conv, slot, active)
        input_grads = place(input_grads, downstream, slot, active)
        if tick < tick_total - 1:
            received = shifted(downstream, "section", -1)

    all_up = lax.all_gather(up_store, "dp", axis=1, tiled=True)
    all_q = lax.all_gather(q_store, "dp", axis=1, tiled=True)
    gains = lax.all_gather(jnp.concatenate([gain_c, gain_p]), "dp", axis=0, tiled=False)
    gains = jnp.sum(gains, axis=0) * norm_scale
    share_gc = lax.dynamic_slice_in_dim(
        gains, dp_index * (channels // group_size), channels // group_size, 0
    )
    share_gp = lax.dynamic_slice_in_dim(
        gains, channels + dp_index * (inner // group_size), inner // group_size, 0
    )

    def in_order(blocks):
        blocks = blocks.reshape(group_size, micro_count, positions, blocks.shape[-1])
        return blocks.transpose(1, 0, 2, 3).reshape(rows, blocks.shape[-1])

    share_conv = contract_rows(in_order(own_columns), all_q.reshape(rows, inner))
    share_point = contract_rows(in_order(own_mix), all_up.reshape(rows, channels))
    return (
        (share_conv * norm_scale)[None],
        (share_point * norm_scale)[None],
        share_gc[None],
        share_gp[None],
        input_grads[None],
    )


def solution(mesh):
    return jax.shard_map(
        on_device,
        mesh=mesh,
        in_specs=(
            P(None, "dp", None),
            P(None, "dp", None),
            P("section", None, None),
            P("section", None, None),
            P("section", None),
            P("section", None),
        ),
        out_specs=(
            P("section", "dp", None),
            P("section", "dp", None),
            P("section", "dp"),
            P("section", "dp"),
            P("section", None, "dp", None),
        ),
        check_vma=False,
    )
```

```python
import functools
import math

import jax
import jax.numpy as jnp
from jax import lax
from jax.experimental import pallas as pl
from jax.experimental.pallas import tpu as pltpu
from jax.sharding import PartitionSpec as P

EPSILON = 1e-06
MESH = pl.DeviceIdType.MESH
GELU_C = math.sqrt(2.0 / math.pi)


def normed(values):
    mean_sq = jnp.mean(values * values, axis=-1, keepdims=True)
    rate = lax.rsqrt(mean_sq + EPSILON)
    return values * rate, rate


def gelu(u):
    return 0.5 * u * (1.0 + jnp.tanh(GELU_C * (u + 0.044715 * u * u * u)))


def act_pull(values, gain, upstream):
    unit, rate = normed(values)
    u = unit * gain
    square = u * u
    bent = jnp.tanh(GELU_C * (u + 0.044715 * square * u))
    slope = 0.5 * (1.0 + bent) + 0.5 * u * (1.0 - bent * bent) * GELU_C * (
        1.0 + 3.0 * 0.044715 * square
    )
    inner = upstream * slope
    grad_gain = jnp.sum(inner * unit, axis=0, keepdims=True)
    scaled = inner * gain
    drift = jnp.mean(scaled * unit, axis=-1, keepdims=True)
    return rate * (scaled - unit * drift), grad_gain


def dot(left, right):
    return jnp.dot(left, right, preferred_element_type=jnp.float32)


def dot_nt(left, right):
    return lax.dot_general(
        left, right, (((1,), (1,)), ((), ())), preferred_element_type=jnp.float32
    )


def dot_tn(left, right):
    return lax.dot_general(
        left, right, (((0,), (0,)), ((), ())), preferred_element_type=jnp.float32
    )


def pick(rows, source_rows, offset):
    row = lax.broadcasted_iota(jnp.int32, (rows, source_rows), 0)
    column = lax.broadcasted_iota(jnp.int32, (rows, source_rows), 1)
    return jnp.where(column - row == offset, 1.0, 0.0).astype(jnp.bfloat16)


def window(share):
    most = max((share * j) % 128 for j in range(128))
    return -(-(share + most) // 128) * 128


def tower(
    sections, group, halo,
    inputs, grad_out, w_conv, w_point, gain_conv, gain_point,
    grads, acts_all, q_all, point_all, gains_all,
    h_in, h_out, e_in, conv, mix, columns, q_own, halo_a, halo_q, point_sum, point_own, gains,
    sec_send, sec_recv, halo_send, halo_recv,
    acts_send, acts_recv, q_send, q_recv, point_send, point_recv, gains_send, gains_recv, own_sem,
):
    section = lax.axis_index("section")
    me = lax.axis_index("dp")
    micros, positions, channels = inputs.shape
    inner = w_conv.shape[1]
    share = 3 * channels // group
    wide = window(share)
    first, last = section == 0, section == sections - 1
    left_end, right_end = me == 0, me == group - 1

    dilation = jnp.int32(1)
    for index in range(sections):
        dilation = jnp.where(section == index, 3**index // 2**index, dilation)

    halo_a[...] = jnp.zeros_like(halo_a)
    halo_q[...] = jnp.zeros_like(halo_q)
    gains[...] = jnp.zeros_like(gains)
    point_sum[...] = jnp.zeros_like(point_sum)

    barrier = pltpu.get_barrier_semaphore()

    def greet(off, carry):
        pl.semaphore_signal(
            barrier, inc=1, device_id={"dp": lax.rem(me + off, group)}, device_id_type=MESH
        )
        return carry

    lax.fori_loop(1, group, greet, 0)

    @pl.when(jnp.logical_not(first))
    def _():
        pl.semaphore_signal(barrier, inc=1, device_id={"section": section - 1}, device_id_type=MESH)

    @pl.when(jnp.logical_not(last))
    def _():
        pl.semaphore_signal(barrier, inc=1, device_id={"section": section + 1}, device_id_type=MESH)

    beside = jnp.where(first, 0, 1) + jnp.where(last, 0, 1)
    pl.semaphore_wait(barrier, group - 1 + beside)

    def remote(src, dst, send, recv, device):
        return pltpu.make_async_remote_copy(
            src_ref=src, dst_ref=dst, send_sem=send, recv_sem=recv,
            device_id=device, device_id_type=MESH,
        )

    def forward_copy(m):
        return remote(
            h_out.at[m], h_in.at[m], sec_send.at[0, m], sec_recv.at[0, m], {"section": section + 1}
        )

    def backward_copy(m):
        return remote(
            grads.at[m], e_in.at[m], sec_send.at[1, m], sec_recv.at[1, m], {"section": section - 1}
        )

    def halo_copy(kind, m, side):
        rows = pl.ds(positions - halo, halo) if side == 0 else pl.ds(0, halo)
        if kind == 0:
            src, store = columns.at[m, rows, pl.ds(channels, channels)], halo_a
        else:
            src, store = q_own.at[m, rows], halo_q
        return remote(
            src, store.at[m, side], halo_send.at[kind, m, side], halo_recv.at[kind, m, side],
            {"dp": me + 1 if side == 0 else me - 1},
        )

    def start_halos(kind, m):
        @pl.when(jnp.logical_not(right_end))
        def _():
            halo_copy(kind, m, 0).start()

        @pl.when(jnp.logical_not(left_end))
        def _():
            halo_copy(kind, m, 1).start()

    def wait_halos(kind, m):
        @pl.when(jnp.logical_not(left_end))
        def _():
            halo_copy(kind, m, 0).wait_recv()

        @pl.when(jnp.logical_not(right_end))
        def _():
            halo_copy(kind, m, 1).wait_recv()

    def wait_halo_sends(kind, m):
        @pl.when(jnp.logical_not(right_end))
        def _():
            halo_copy(kind, m, 0).wait_send()

        @pl.when(jnp.logical_not(left_end))
        def _():
            halo_copy(kind, m, 1).wait_send()

    def acts_part(m, owner):
        start = pl.multiple_of((share * owner) // 128 * 128, 128)
        return columns.at[m, :, pl.ds(start, wide)]

    def acts_copy(m, off):
        peer = lax.rem(me + off, group)
        return remote(
            acts_part(m, peer), acts_all.at[me, m], acts_send.at[m, off], acts_recv.at[m, off],
            {"dp": peer},
        )

    def q_copy(m, off):
        peer = lax.rem(me + off, group)
        return remote(
            q_own.at[m], q_all.at[me, m], q_send.at[m, off], q_recv.at[m, off], {"dp": peer}
        )

    def point_copy(off):
        peer = lax.rem(me + off, group)
        return remote(
            point_own.at[peer], point_all.at[me], point_send.at[off], point_recv.at[off],
            {"dp": peer},
        )

    def gains_copy(off):
        peer = lax.rem(me + off, group)
        return remote(
            gains, gains_all.at[me], gains_send.at[off], gains_recv.at[off], {"dp": peer}
        )

    def each_peer(action):
        def step(off, carry):
            action(off)
            return carry

        lax.fori_loop(1, group, step, 0)

    def earlier_of(own, store):
        return (
            dot(pick(positions, positions, -dilation), own)
            + dot(pick(positions, halo, halo - dilation), store)
        ).astype(jnp.bfloat16)

    def later_of(own, store):
        return (
            dot(pick(positions, positions, dilation), own)
            + dot(pick(positions, halo, dilation - positions), store)
        ).astype(jnp.bfloat16)

    def forward(m, carry):
        @pl.when(first)
        def _():
            h_in[m] = inputs[m]

        @pl.when(jnp.logical_not(first))
        def _():
            forward_copy(m).wait_recv()

        unit, _unused = normed(h_in[m].astype(jnp.float32))
        own = gelu(unit * gain_conv[...]).astype(jnp.bfloat16)
        columns[m, :, channels : 2 * channels] = own
        start_halos(0, m)
        total = dot(own, w_conv[channels : 2 * channels])
        wait_halos(0, m)
        earlier = earlier_of(own, halo_a[m, 0])
        columns[m, :, :channels] = earlier
        total = total + dot(earlier, w_conv[:channels])
        later = later_of(own, halo_a[m, 1])
        columns[m, :, 2 * channels :] = later
        total = total + dot(later, w_conv[2 * channels :])
        conv[m] = total
        unit, _unused = normed(total)
        mixture = gelu(unit * gain_point[...]).astype(jnp.bfloat16)
        mix[m] = mixture

        @pl.when(jnp.logical_not(last))
        def _():
            branch = dot(mix[m], w_point[...])
            h_out[m] = (h_in[m].astype(jnp.float32) + branch).astype(jnp.bfloat16)
            forward_copy(m).start()

        each_peer(lambda off: acts_copy(m, off).start())
        return carry

    lax.fori_loop(0, micros, forward, 0)

    def backward(m, carry):
        @pl.when(last)
        def _():
            e_in[m] = grad_out[m]

        @pl.when(jnp.logical_not(last))
        def _():
            backward_copy(m).wait_recv()

        grad_mix = dot_nt(e_in[m], w_point[...])
        grad_conv, grad_gain = act_pull(conv[m], gain_point[...], grad_mix)
        gains[:, channels:] += grad_gain
        own = grad_conv.astype(jnp.bfloat16)
        q_own[m] = own
        start_halos(1, m)
        back = dot_nt(own, w_conv[channels : 2 * channels])
        wait_halos(1, m)
        back = back + dot_nt(later_of(own, halo_q[m, 1]), w_conv[:channels])
        back = back + dot_nt(earlier_of(own, halo_q[m, 0]), w_conv[2 * channels :])
        grad_in, grad_gain = act_pull(h_in[m].astype(jnp.float32), gain_conv[...], back)
        gains[:, :channels] += grad_gain
        grads[m] = (e_in[m].astype(jnp.float32) + grad_in).astype(jnp.bfloat16)

        @pl.when(jnp.logical_not(first))
        def _():
            backward_copy(m).start()

        each_peer(lambda off: q_copy(m, off).start())
        point_sum[...] += dot_tn(mix[m], e_in[m])
        return carry

    lax.fori_loop(0, micros, backward, 0)

    rows = inner // group
    for owner in range(group):
        point_own[owner] = point_sum[owner * rows : (owner + 1) * rows].astype(jnp.bfloat16)
    each_peer(lambda off: gains_copy(off).start())
    each_peer(lambda off: point_copy(off).start())

    own_copies = [
        pltpu.make_async_copy(point_own.at[me], point_all.at[me], own_sem.at[0]),
        pltpu.make_async_copy(gains, gains_all.at[me], own_sem.at[1]),
    ]
    for m in range(micros):
        own_copies += [
            pltpu.make_async_copy(acts_part(m, me), acts_all.at[me, m], own_sem.at[2 + 2 * m]),
            pltpu.make_async_copy(q_own.at[m], q_all.at[me, m], own_sem.at[3 + 2 * m]),
        ]
    for copy in own_copies:
        copy.start()
    for copy in own_copies:
        copy.wait()

    def finish(m, carry):
        for kind in range(2):
            wait_halo_sends(kind, m)

        @pl.when(jnp.logical_not(last))
        def _():
            forward_copy(m).wait_send()

        @pl.when(jnp.logical_not(first))
        def _():
            backward_copy(m).wait_send()

        each_peer(lambda off: acts_copy(m, off).wait())
        each_peer(lambda off: q_copy(m, off).wait())
        return carry

    lax.fori_loop(0, micros, finish, 0)
    each_peer(lambda off: gains_copy(off).wait())
    each_peer(lambda off: point_copy(off).wait())


def on_device(inputs, grad_out, w_conv, w_point, gain_conv, gain_point):
    micros, positions, channels = inputs.shape
    sections, group = lax.axis_size("section"), lax.axis_size("dp")
    me = lax.axis_index("dp")
    inner = w_conv.shape[2]
    norm_scale = 1.0 / math.sqrt(micros * positions * group)
    reach = 3 ** (sections - 1) // 2 ** (sections - 1)
    halo = -(-reach // 16) * 16
    share, rows = 3 * channels // group, inner // group
    wide = window(share)
    bf16, f32 = jnp.bfloat16, jnp.float32
    dma = pltpu.SemaphoreType.DMA
    vmem = pl.BlockSpec(memory_space=pltpu.VMEM)
    anywhere = pl.BlockSpec(memory_space=pl.ANY)
    with jax.named_scope("tower"):
        grads, acts_all, q_all, point_all, gains_all = pl.pallas_call(
            functools.partial(tower, sections, group, halo),
            out_shape=[
                jax.ShapeDtypeStruct(inputs.shape, bf16),
                jax.ShapeDtypeStruct((group, micros, positions, wide), bf16),
                jax.ShapeDtypeStruct((group, micros, positions, inner), bf16),
                jax.ShapeDtypeStruct((group, rows, channels), bf16),
                jax.ShapeDtypeStruct((group, 1, channels + inner), f32),
            ],
            in_specs=[vmem] * 6,
            out_specs=[vmem] + [anywhere] * 4,
            scratch_shapes=[
                pltpu.VMEM((micros, positions, channels), bf16),
                pltpu.VMEM((micros, positions, channels), bf16),
                pltpu.VMEM((micros, positions, channels), bf16),
                pltpu.VMEM((micros, positions, inner), f32),
                pltpu.VMEM((micros, positions, inner), bf16),
                pltpu.VMEM((micros, positions, 3 * channels), bf16),
                pltpu.VMEM((micros, positions, inner), bf16),
                pltpu.VMEM((micros, 2, halo, channels), bf16),
                pltpu.VMEM((micros, 2, halo, inner), bf16),
                pltpu.VMEM((inner, channels), f32),
                pltpu.VMEM((group, rows, channels), bf16),
                pltpu.VMEM((1, channels + inner), f32),
                dma((2, micros)), dma((2, micros)),
                dma((2, micros, 2)), dma((2, micros, 2)),
                dma((micros, group)), dma((micros, group)),
                dma((micros, group)), dma((micros, group)),
                dma((group,)), dma((group,)),
                dma((group,)), dma((group,)),
                dma((2 + 2 * micros,)),
            ],
            compiler_params=pltpu.CompilerParams(
                collective_id=0, has_side_effects=True, vmem_limit_bytes=56 * 2**20
            ),
        )(inputs, grad_out, w_conv[0], w_point[0], gain_conv, gain_point)

    total = group * micros * positions
    conv_rows = lax.dot_general(
        acts_all.reshape(total, wide), q_all.reshape(total, inner),
        (((0,), (0,)), ((), ())), preferred_element_type=f32,
    )
    share_conv = lax.dynamic_slice_in_dim(conv_rows, lax.rem(share * me, 128), share, 0)
    share_point = jnp.sum(point_all.astype(f32), axis=0)
    gains = jnp.sum(gains_all, axis=(0, 1))
    own_c, own_p = channels // group, inner // group
    share_gc = lax.dynamic_slice_in_dim(gains, me * own_c, own_c, 0)
    share_gp = lax.dynamic_slice_in_dim(gains, channels + me * own_p, own_p, 0)
    return (
        (share_conv * norm_scale)[None],
        (share_point * norm_scale)[None],
        (share_gc * norm_scale)[None],
        (share_gp * norm_scale)[None],
        grads[None],
    )


def solution(mesh):
    return jax.shard_map(
        on_device,
        mesh=mesh,
        in_specs=(
            P(None, "dp", None),
            P(None, "dp", None),
            P("section", None, None),
            P("section", None, None),
            P("section", None),
            P("section", None),
        ),
        out_specs=(
            P("section", "dp", None),
            P("section", "dp", None),
            P("section", "dp"),
            P("section", "dp"),
            P("section", None, "dp", None),
        ),
        check_vma=False,
    )
```

```python
import functools
import math

import jax
import jax.numpy as jnp
from jax import lax
from jax.experimental import pallas as pl
from jax.experimental.pallas import tpu as pltpu
from jax.sharding import PartitionSpec as P

EPSILON = 1e-06
MESH = pl.DeviceIdType.MESH
GELU_C = math.sqrt(2.0 / math.pi)


def normed(values):
    mean_sq = jnp.mean(values * values, axis=-1, keepdims=True)
    rate = lax.rsqrt(mean_sq + EPSILON)
    return values * rate, rate


def gelu(u):
    return 0.5 * u * (1.0 + jnp.tanh(GELU_C * (u + 0.044715 * u * u * u)))


def act_pull(values, gain, upstream):
    unit, rate = normed(values)
    u = unit * gain
    square = u * u
    bent = jnp.tanh(GELU_C * (u + 0.044715 * square * u))
    slope = 0.5 * (1.0 + bent) + 0.5 * u * (1.0 - bent * bent) * GELU_C * (
        1.0 + 3.0 * 0.044715 * square
    )
    inner = upstream * slope
    grad_gain = jnp.sum(inner * unit, axis=0, keepdims=True)
    scaled = inner * gain
    drift = jnp.mean(scaled * unit, axis=-1, keepdims=True)
    return rate * (scaled - unit * drift), grad_gain


def dot(left, right):
    return jnp.dot(left, right, preferred_element_type=jnp.float32)


def dot_nt(left, right):
    return lax.dot_general(
        left, right, (((1,), (1,)), ((), ())), preferred_element_type=jnp.float32
    )


def dot_tn(left, right):
    return lax.dot_general(
        left, right, (((0,), (0,)), ((), ())), preferred_element_type=jnp.float32
    )


def pick(rows, source_rows, offset):
    row = lax.broadcasted_iota(jnp.int32, (rows, source_rows), 0)
    column = lax.broadcasted_iota(jnp.int32, (rows, source_rows), 1)
    return jnp.where(column - row == offset, 1.0, 0.0).astype(jnp.bfloat16)


def window(share):
    most = max((share * j) % 128 for j in range(128))
    return -(-(share + most) // 128) * 128


def tower(
    sections, group, halo,
    inputs, grad_out, w_conv, w_point, gain_conv, gain_point,
    grads, acts_all, q_all, point_all, gains_all,
    h_in, h_out, e_in, conv, mix, columns, q_own, halo_a, halo_q, point_sum, pair_out, pair_in,
    point_out, gains,
    sec_send, sec_recv, halo_send, halo_recv,
    acts_send, acts_recv, q_send, q_recv, pass_send, pass_recv, pair_send, pair_recv,
    point_send, point_recv, gains_send, gains_recv, own_sem,
):
    section = lax.axis_index("section")
    me = lax.axis_index("dp")
    micros, positions, channels = inputs.shape
    inner = w_conv.shape[1]
    share = 3 * channels // group
    wide = window(share)
    first, last = section == 0, section == sections - 1
    left_end, right_end = me == 0, me == group - 1
    half = group // 2
    parity, spot = lax.rem(me, 2), me // 2
    partner = me + 1 - 2 * parity
    rows = inner // group

    dilation = jnp.int32(1)
    for index in range(sections):
        dilation = jnp.where(section == index, 3**index // 2**index, dilation)

    halo_a[...] = jnp.zeros_like(halo_a)
    halo_q[...] = jnp.zeros_like(halo_q)
    gains[...] = jnp.zeros_like(gains)
    point_sum[...] = jnp.zeros_like(point_sum)

    barrier = pltpu.get_barrier_semaphore()

    def greet(off, carry):
        pl.semaphore_signal(
            barrier, inc=1, device_id={"dp": lax.rem(me + off, group)}, device_id_type=MESH
        )
        return carry

    lax.fori_loop(1, group, greet, 0)

    @pl.when(jnp.logical_not(first))
    def _():
        pl.semaphore_signal(barrier, inc=1, device_id={"section": section - 1}, device_id_type=MESH)

    @pl.when(jnp.logical_not(last))
    def _():
        pl.semaphore_signal(barrier, inc=1, device_id={"section": section + 1}, device_id_type=MESH)

    beside = jnp.where(first, 0, 1) + jnp.where(last, 0, 1)
    pl.semaphore_wait(barrier, group - 1 + beside)

    def remote(src, dst, send, recv, device):
        return pltpu.make_async_remote_copy(
            src_ref=src, dst_ref=dst, send_sem=send, recv_sem=recv,
            device_id=device, device_id_type=MESH,
        )

    def forward_copy(m):
        return remote(
            h_out.at[m], h_in.at[m], sec_send.at[0, m], sec_recv.at[0, m], {"section": section + 1}
        )

    def backward_copy(m):
        return remote(
            grads.at[m], e_in.at[m], sec_send.at[1, m], sec_recv.at[1, m], {"section": section - 1}
        )

    def halo_copy(kind, m, side):
        rows = pl.ds(positions - halo, halo) if side == 0 else pl.ds(0, halo)
        if kind == 0:
            src, store = columns.at[m, rows, pl.ds(channels, channels)], halo_a
        else:
            src, store = q_own.at[m, rows], halo_q
        return remote(
            src, store.at[m, side], halo_send.at[kind, m, side], halo_recv.at[kind, m, side],
            {"dp": me + 1 if side == 0 else me - 1},
        )

    def start_halos(kind, m):
        @pl.when(jnp.logical_not(right_end))
        def _():
            halo_copy(kind, m, 0).start()

        @pl.when(jnp.logical_not(left_end))
        def _():
            halo_copy(kind, m, 1).start()

    def wait_halos(kind, m):
        @pl.when(jnp.logical_not(left_end))
        def _():
            halo_copy(kind, m, 0).wait_recv()

        @pl.when(jnp.logical_not(right_end))
        def _():
            halo_copy(kind, m, 1).wait_recv()

    def wait_halo_sends(kind, m):
        @pl.when(jnp.logical_not(right_end))
        def _():
            halo_copy(kind, m, 0).wait_send()

        @pl.when(jnp.logical_not(left_end))
        def _():
            halo_copy(kind, m, 1).wait_send()

    def acts_part(m, owner):
        start = pl.multiple_of((share * owner) // 128 * 128, 128)
        return columns.at[m, :, pl.ds(start, wide)]

    def acts_copy(m, off):
        peer = lax.rem(me + off, group)
        return remote(
            acts_part(m, peer), acts_all.at[me, m], acts_send.at[m, off], acts_recv.at[m, off],
            {"dp": peer},
        )

    def column_peer(off):
        return 2 * lax.rem(spot + off, half) + parity

    def q_copy(m, off):
        return remote(
            q_own.at[m], q_all.at[me, m], q_send.at[m, off], q_recv.at[m, off],
            {"dp": column_peer(off)},
        )

    def pass_copy(m, off):
        source = 2 * lax.rem(spot - off + half, half) + parity
        return remote(
            q_all.at[source, m], q_all.at[source, m], pass_send.at[m, off], pass_recv.at[m, off],
            {"dp": partner},
        )

    def own_pass_copy(m):
        return remote(
            q_own.at[m], q_all.at[me, m], pass_send.at[m, 0], pass_recv.at[m, 0],
            {"dp": partner},
        )

    def pair_copy(i):
        return remote(
            pair_out.at[i], pair_in.at[i], pair_send.at[i], pair_recv.at[i], {"dp": partner}
        )

    def point_copy(off):
        return remote(
            point_out.at[lax.rem(spot + off, half)], point_all.at[spot],
            point_send.at[off], point_recv.at[off], {"dp": column_peer(off)},
        )

    def gains_copy(off):
        peer = lax.rem(me + off, group)
        return remote(
            gains, gains_all.at[me], gains_send.at[off], gains_recv.at[off], {"dp": peer}
        )

    def each_peer(action):
        def step(off, carry):
            action(off)
            return carry

        lax.fori_loop(1, group, step, 0)

    def each_column_peer(action):
        def step(off, carry):
            action(off)
            return carry

        lax.fori_loop(1, half, step, 0)

    def pass_on(m):
        def step(off):
            q_copy(m, off).wait_recv()
            pass_copy(m, off).start()

        each_column_peer(step)

    def start_acts():
        def step(m, carry):
            each_peer(lambda off: acts_copy(m, off).start())
            return carry

        lax.fori_loop(0, micros, step, 0)

    def earlier_of(own, store):
        return (
            dot(pick(positions, positions, -dilation), own)
            + dot(pick(positions, halo, halo - dilation), store)
        ).astype(jnp.bfloat16)

    def later_of(own, store):
        return (
            dot(pick(positions, positions, dilation), own)
            + dot(pick(positions, halo, dilation - positions), store)
        ).astype(jnp.bfloat16)

    def forward(m, carry):
        @pl.when(first)
        def _():
            h_in[m] = inputs[m]

        @pl.when(jnp.logical_not(first))
        def _():
            forward_copy(m).wait_recv()

        unit, _unused = normed(h_in[m].astype(jnp.float32))
        own = gelu(unit * gain_conv[...]).astype(jnp.bfloat16)
        columns[m, :, channels : 2 * channels] = own
        start_halos(0, m)
        total = dot(own, w_conv[channels : 2 * channels])
        wait_halos(0, m)
        earlier = earlier_of(own, halo_a[m, 0])
        columns[m, :, :channels] = earlier
        total = total + dot(earlier, w_conv[:channels])
        later = later_of(own, halo_a[m, 1])
        columns[m, :, 2 * channels :] = later
        total = total + dot(later, w_conv[2 * channels :])
        conv[m] = total
        unit, _unused = normed(total)
        mixture = gelu(unit * gain_point[...]).astype(jnp.bfloat16)
        mix[m] = mixture

        @pl.when(jnp.logical_not(last))
        def _():
            branch = dot(mix[m], w_point[...])
            h_out[m] = (h_in[m].astype(jnp.float32) + branch).astype(jnp.bfloat16)
            forward_copy(m).start()

        return carry

    lax.fori_loop(0, micros, forward, 0)

    @pl.when(jnp.logical_not(last))
    def _():
        start_acts()

    def backward(m, carry):
        @pl.when(last)
        def _():
            e_in[m] = grad_out[m]

        @pl.when(jnp.logical_not(last))
        def _():
            backward_copy(m).wait_recv()

        grad_mix = dot_nt(e_in[m], w_point[...])
        grad_conv, grad_gain = act_pull(conv[m], gain_point[...], grad_mix)
        gains[:, channels:] += grad_gain
        own = grad_conv.astype(jnp.bfloat16)
        q_own[m] = own
        start_halos(1, m)
        back = dot_nt(own, w_conv[channels : 2 * channels])
        wait_halos(1, m)
        back = back + dot_nt(later_of(own, halo_q[m, 1]), w_conv[:channels])
        back = back + dot_nt(earlier_of(own, halo_q[m, 0]), w_conv[2 * channels :])
        grad_in, grad_gain = act_pull(h_in[m].astype(jnp.float32), gain_conv[...], back)
        gains[:, :channels] += grad_gain
        grads[m] = (e_in[m].astype(jnp.float32) + grad_in).astype(jnp.bfloat16)

        @pl.when(jnp.logical_not(first))
        def _():
            backward_copy(m).start()

        each_column_peer(lambda off: q_copy(m, off).start())
        own_pass_copy(m).start()

        @pl.when(m > 0)
        def _():
            pass_on(m - 1)

        point_sum[...] += dot_tn(mix[m], e_in[m])
        return carry

    lax.fori_loop(0, micros, backward, 0)

    def block(i, side):
        start = pl.multiple_of((2 * i + side) * rows, 8)
        return point_sum[pl.ds(start, rows), :]

    def send_pair(i, carry):
        pair_out[i] = block(i, 1 - parity).astype(jnp.bfloat16)
        pair_copy(i).start()
        return carry

    lax.fori_loop(0, half, send_pair, 0)
    each_peer(lambda off: gains_copy(off).start())
    pass_on(micros - 1)

    def add_pair(i, carry):
        pair_copy(i).wait_recv()
        point_out[i] = (block(i, parity) + pair_in[i].astype(jnp.float32)).astype(jnp.bfloat16)
        return carry

    lax.fori_loop(0, half, add_pair, 0)
    each_column_peer(lambda off: point_copy(off).start())

    @pl.when(last)
    def _():
        start_acts()

    own_copies = [
        pltpu.make_async_copy(point_out.at[spot], point_all.at[spot], own_sem.at[0]),
        pltpu.make_async_copy(gains, gains_all.at[me], own_sem.at[1]),
    ]
    for m in range(micros):
        own_copies += [
            pltpu.make_async_copy(acts_part(m, me), acts_all.at[me, m], own_sem.at[2 + 2 * m]),
            pltpu.make_async_copy(q_own.at[m], q_all.at[me, m], own_sem.at[3 + 2 * m]),
        ]
    for copy in own_copies:
        copy.start()
    for copy in own_copies:
        copy.wait()

    def finish(m, carry):
        for kind in range(2):
            wait_halo_sends(kind, m)

        @pl.when(jnp.logical_not(last))
        def _():
            forward_copy(m).wait_send()

        @pl.when(jnp.logical_not(first))
        def _():
            backward_copy(m).wait_send()

        each_peer(lambda off: acts_copy(m, off).wait())
        each_column_peer(lambda off: q_copy(m, off).wait_send())
        own_pass_copy(m).wait()
        each_column_peer(lambda off: pass_copy(m, off).wait())
        return carry

    lax.fori_loop(0, micros, finish, 0)
    each_peer(lambda off: gains_copy(off).wait())
    each_column_peer(lambda off: point_copy(off).wait())

    def finish_pair(i, carry):
        pair_copy(i).wait_send()
        return carry

    lax.fori_loop(0, half, finish_pair, 0)


def on_device(inputs, grad_out, w_conv, w_point, gain_conv, gain_point):
    micros, positions, channels = inputs.shape
    sections, group = lax.axis_size("section"), lax.axis_size("dp")
    me = lax.axis_index("dp")
    inner = w_conv.shape[2]
    norm_scale = 1.0 / math.sqrt(micros * positions * group)
    reach = 3 ** (sections - 1) // 2 ** (sections - 1)
    halo = -(-reach // 16) * 16
    share, rows = 3 * channels // group, inner // group
    wide = window(share)
    half = group // 2
    bf16, f32 = jnp.bfloat16, jnp.float32
    dma = pltpu.SemaphoreType.DMA
    vmem = pl.BlockSpec(memory_space=pltpu.VMEM)
    anywhere = pl.BlockSpec(memory_space=pl.ANY)
    with jax.named_scope("tower"):
        grads, acts_all, q_all, point_all, gains_all = pl.pallas_call(
            functools.partial(tower, sections, group, halo),
            out_shape=[
                jax.ShapeDtypeStruct(inputs.shape, bf16),
                jax.ShapeDtypeStruct((group, micros, positions, wide), bf16),
                jax.ShapeDtypeStruct((group, micros, positions, inner), bf16),
                jax.ShapeDtypeStruct((half, rows, channels), bf16),
                jax.ShapeDtypeStruct((group, 1, channels + inner), f32),
            ],
            in_specs=[vmem] * 6,
            out_specs=[vmem] + [anywhere] * 4,
            scratch_shapes=[
                pltpu.VMEM((micros, positions, channels), bf16),
                pltpu.VMEM((micros, positions, channels), bf16),
                pltpu.VMEM((micros, positions, channels), bf16),
                pltpu.VMEM((micros, positions, inner), f32),
                pltpu.VMEM((micros, positions, inner), bf16),
                pltpu.VMEM((micros, positions, 3 * channels), bf16),
                pltpu.VMEM((micros, positions, inner), bf16),
                pltpu.VMEM((micros, 2, halo, channels), bf16),
                pltpu.VMEM((micros, 2, halo, inner), bf16),
                pltpu.VMEM((inner, channels), f32),
                pltpu.VMEM((half, rows, channels), bf16),
                pltpu.VMEM((half, rows, channels), bf16),
                pltpu.VMEM((half, rows, channels), bf16),
                pltpu.VMEM((1, channels + inner), f32),
                dma((2, micros)), dma((2, micros)),
                dma((2, micros, 2)), dma((2, micros, 2)),
                dma((micros, group)), dma((micros, group)),
                dma((micros, half)), dma((micros, half)),
                dma((micros, half)), dma((micros, half)),
                dma((half,)), dma((half,)),
                dma((half,)), dma((half,)),
                dma((group,)), dma((group,)),
                dma((2 + 2 * micros,)),
            ],
            compiler_params=pltpu.CompilerParams(
                collective_id=0, has_side_effects=True, vmem_limit_bytes=56 * 2**20
            ),
        )(inputs, grad_out, w_conv[0], w_point[0], gain_conv, gain_point)

    total = group * micros * positions
    conv_rows = lax.dot_general(
        acts_all.reshape(total, wide), q_all.reshape(total, inner),
        (((0,), (0,)), ((), ())), preferred_element_type=f32,
    )
    share_conv = lax.dynamic_slice_in_dim(conv_rows, lax.rem(share * me, 128), share, 0)
    share_point = jnp.sum(point_all.astype(f32), axis=0)
    gains = jnp.sum(gains_all, axis=(0, 1))
    own_c, own_p = channels // group, inner // group
    share_gc = lax.dynamic_slice_in_dim(gains, me * own_c, own_c, 0)
    share_gp = lax.dynamic_slice_in_dim(gains, channels + me * own_p, own_p, 0)
    return (
        (share_conv * norm_scale)[None],
        (share_point * norm_scale)[None],
        (share_gc * norm_scale)[None],
        (share_gp * norm_scale)[None],
        grads[None],
    )


def solution(mesh):
    return jax.shard_map(
        on_device,
        mesh=mesh,
        in_specs=(
            P(None, "dp", None),
            P(None, "dp", None),
            P("section", None, None),
            P("section", None, None),
            P("section", None),
            P("section", None),
        ),
        out_specs=(
            P("section", "dp", None),
            P("section", "dp", None),
            P("section", "dp"),
            P("section", "dp"),
            P("section", None, "dp", None),
        ),
        check_vma=False,
    )
```

```python
import functools
import math

import jax
import jax.numpy as jnp
from jax import lax
from jax.experimental import pallas as pl
from jax.experimental.pallas import tpu as pltpu
from jax.sharding import PartitionSpec as P

EPSILON = 1e-06
MESH = pl.DeviceIdType.MESH
GELU_C = math.sqrt(2.0 / math.pi)


def normed(values):
    mean_sq = jnp.mean(values * values, axis=-1, keepdims=True)
    rate = lax.rsqrt(mean_sq + EPSILON)
    return values * rate, rate


def gelu(u):
    return 0.5 * u * (1.0 + jnp.tanh(GELU_C * (u + 0.044715 * u * u * u)))


def act_pull(values, gain, upstream):
    unit, rate = normed(values)
    u = unit * gain
    square = u * u
    bent = jnp.tanh(GELU_C * (u + 0.044715 * square * u))
    slope = 0.5 * (1.0 + bent) + 0.5 * u * (1.0 - bent * bent) * GELU_C * (
        1.0 + 3.0 * 0.044715 * square
    )
    inner = upstream * slope
    grad_gain = jnp.sum(inner * unit, axis=0, keepdims=True)
    scaled = inner * gain
    drift = jnp.mean(scaled * unit, axis=-1, keepdims=True)
    return rate * (scaled - unit * drift), grad_gain


def dot(left, right):
    return jnp.dot(left, right, preferred_element_type=jnp.float32)


def dot_nt(left, right):
    return lax.dot_general(
        left, right, (((1,), (1,)), ((), ())), preferred_element_type=jnp.float32
    )


def dot_tn(left, right):
    return lax.dot_general(
        left, right, (((0,), (0,)), ((), ())), preferred_element_type=jnp.float32
    )


def pick(rows, source_rows, offset):
    row = lax.broadcasted_iota(jnp.int32, (rows, source_rows), 0)
    column = lax.broadcasted_iota(jnp.int32, (rows, source_rows), 1)
    return jnp.where(column - row == offset, 1.0, 0.0).astype(jnp.bfloat16)


def window(share):
    most = max((share * j) % 128 for j in range(128))
    return -(-(share + most) // 128) * 128


def tower(
    sections, group, halo,
    inputs, grad_out, w_conv, w_point, gain_conv, gain_point,
    grads, acts_all, q_all, point_all, gains_all,
    h_in, h_out, e_in, conv, mix, columns, q_own, halo_a, halo_q, point_sum, pair_out, pair_in,
    point_out, gains,
    sec_send, sec_recv, halo_send, halo_recv,
    acts_send, acts_recv, q_send, q_recv, pass_send, pass_recv, pair_send, pair_recv,
    point_send, point_recv, gains_send, gains_recv, own_sem,
):
    section = lax.axis_index("section")
    me = lax.axis_index("dp")
    micros, positions, channels = inputs.shape
    inner = w_conv.shape[1]
    share = 3 * channels // group
    wide = window(share)
    first, last = section == 0, section == sections - 1
    left_end, right_end = me == 0, me == group - 1
    half = group // 2
    parity, spot = lax.rem(me, 2), me // 2
    partner = me + 1 - 2 * parity
    rows = inner // group

    dilation = jnp.int32(1)
    for index in range(sections):
        dilation = jnp.where(section == index, 3**index // 2**index, dilation)

    halo_a[...] = jnp.zeros_like(halo_a)
    halo_q[...] = jnp.zeros_like(halo_q)
    gains[...] = jnp.zeros_like(gains)

    barrier = pltpu.get_barrier_semaphore()

    def greet(off, carry):
        pl.semaphore_signal(
            barrier, inc=1, device_id={"dp": lax.rem(me + off, group)}, device_id_type=MESH
        )
        return carry

    lax.fori_loop(1, group, greet, 0)

    @pl.when(jnp.logical_not(first))
    def _():
        pl.semaphore_signal(barrier, inc=1, device_id={"section": section - 1}, device_id_type=MESH)

    @pl.when(jnp.logical_not(last))
    def _():
        pl.semaphore_signal(barrier, inc=1, device_id={"section": section + 1}, device_id_type=MESH)

    def greet_diagonal(there, step, by):
        @pl.when(jnp.logical_and(there, jnp.logical_not(left_end if step < 0 else right_end)))
        def _():
            pl.semaphore_signal(
                barrier, inc=1, device_id={"section": section + by, "dp": me + step},
                device_id_type=MESH,
            )

    for step in (-1, 1):
        greet_diagonal(jnp.logical_not(first), step, -1)
        greet_diagonal(jnp.logical_not(last), step, 1)
    beside = jnp.where(first, 0, 1) + jnp.where(last, 0, 1)
    ends = jnp.where(left_end, 0, 1) + jnp.where(right_end, 0, 1)
    pl.semaphore_wait(barrier, group - 1 + beside * (1 + ends))

    def remote(src, dst, send, recv, device):
        return pltpu.make_async_remote_copy(
            src_ref=src, dst_ref=dst, send_sem=send, recv_sem=recv,
            device_id=device, device_id_type=MESH,
        )

    def forward_copy(m, part):
        place = pl.ds(part * (channels // 2), channels // 2)
        return remote(
            h_out.at[m, :, place], h_in.at[m, :, place],
            sec_send.at[part, m], sec_recv.at[part, m], {"section": section + 1},
        )

    def backward_copy(m):
        return remote(
            grads.at[m], e_in.at[m], sec_send.at[2, m], sec_recv.at[2, m], {"section": section - 1}
        )

    def halo_copy(kind, m, side):
        rows = pl.ds(positions - halo, halo) if side == 0 else pl.ds(0, halo)
        device = {"dp": me + 1 if side == 0 else me - 1}
        if kind == 0:
            src, store = h_out.at[m, rows], halo_a
            device["section"] = section + 1
        elif kind == 1:
            src, store = q_own.at[m, rows], halo_q
        else:
            src, store = inputs.at[m, rows], halo_a
        return remote(
            src, store.at[m, side], halo_send.at[kind, m, side], halo_recv.at[kind % 2, m, side],
            device,
        )

    def start_halos(kind, m):
        @pl.when(jnp.logical_not(right_end))
        def _():
            halo_copy(kind, m, 0).start()

        @pl.when(jnp.logical_not(left_end))
        def _():
            halo_copy(kind, m, 1).start()

    def wait_halos(kind, m):
        @pl.when(jnp.logical_not(left_end))
        def _():
            halo_copy(kind, m, 0).wait_recv()

        @pl.when(jnp.logical_not(right_end))
        def _():
            halo_copy(kind, m, 1).wait_recv()

    def wait_halo_sends(kind, m):
        @pl.when(jnp.logical_not(right_end))
        def _():
            halo_copy(kind, m, 0).wait_send()

        @pl.when(jnp.logical_not(left_end))
        def _():
            halo_copy(kind, m, 1).wait_send()

    def acts_part(m, owner):
        start = pl.multiple_of((share * owner) // 128 * 128, 128)
        return columns.at[m, :, pl.ds(start, wide)]

    def acts_copy(m, off):
        peer = lax.rem(me + off, group)
        return remote(
            acts_part(m, peer), acts_all.at[me, m], acts_send.at[m, off], acts_recv.at[m, off],
            {"dp": peer},
        )

    def column_peer(off):
        return 2 * lax.rem(spot + off, half) + parity

    def q_copy(m, off):
        return remote(
            q_own.at[m], q_all.at[me, m], q_send.at[m, off], q_recv.at[m, off],
            {"dp": column_peer(off)},
        )

    def pass_copy(m, off):
        source = 2 * lax.rem(spot - off + half, half) + parity
        return remote(
            q_all.at[source, m], q_all.at[source, m], pass_send.at[m, off], pass_recv.at[m, off],
            {"dp": partner},
        )

    def own_pass_copy(m):
        return remote(
            q_own.at[m], q_all.at[me, m], pass_send.at[m, 0], pass_recv.at[m, 0],
            {"dp": partner},
        )

    def pair_copy(i):
        return remote(
            pair_out.at[i], pair_in.at[i], pair_send.at[i], pair_recv.at[i], {"dp": partner}
        )

    def point_copy(off):
        return remote(
            point_out.at[lax.rem(spot + off, half)], point_all.at[spot],
            point_send.at[off], point_recv.at[off], {"dp": column_peer(off)},
        )

    def gains_copy(off):
        peer = lax.rem(me + off, group)
        return remote(
            gains, gains_all.at[me], gains_send.at[off], gains_recv.at[off], {"dp": peer}
        )

    def each_peer(action):
        def step(off, carry):
            action(off)
            return carry

        lax.fori_loop(1, group, step, 0)

    def each_column_peer(action):
        def step(off, carry):
            action(off)
            return carry

        lax.fori_loop(1, half, step, 0)

    def pass_on(m):
        def step(off):
            q_copy(m, off).wait_recv()
            pass_copy(m, off).start()

        each_column_peer(step)

    def start_acts():
        def step(m, carry):
            each_peer(lambda off: acts_copy(m, off).start())
            return carry

        lax.fori_loop(0, micros, step, 0)

    def earlier_of(own, store):
        return (
            dot(pick(positions, positions, -dilation), own)
            + dot(pick(positions, halo, halo - dilation), store)
        ).astype(jnp.bfloat16)

    def later_of(own, store):
        return (
            dot(pick(positions, positions, dilation), own)
            + dot(pick(positions, halo, dilation - positions), store)
        ).astype(jnp.bfloat16)

    @pl.when(first)
    def _():
        for m in range(micros):
            start_halos(2, m)

    def forward(m, carry):
        @pl.when(first)
        def _():
            h_in[m] = inputs[m]

        @pl.when(jnp.logical_not(first))
        def _():
            for part in range(2):
                forward_copy(m, part).wait_recv()

        def activated(values):
            unit, _unused = normed(values.astype(jnp.float32))
            return gelu(unit * gain_conv[...]).astype(jnp.bfloat16)

        own = activated(h_in[m])
        columns[m, :, channels : 2 * channels] = own
        total = dot(own, w_conv[channels : 2 * channels])
        wait_halos(0, m)
        earlier = earlier_of(own, activated(halo_a[m, 0]))
        columns[m, :, :channels] = earlier
        total = total + dot(earlier, w_conv[:channels])
        later = later_of(own, activated(halo_a[m, 1]))
        columns[m, :, 2 * channels :] = later
        total = total + dot(later, w_conv[2 * channels :])
        conv[m] = total
        unit, _unused = normed(total)
        mixture = gelu(unit * gain_point[...]).astype(jnp.bfloat16)
        mix[m] = mixture

        @pl.when(jnp.logical_not(last))
        def _():
            for part in range(2):
                place = slice(part * (channels // 2), (part + 1) * (channels // 2))
                branch = dot(mix[m], w_point[:, place])
                h_out[m, :, place] = (
                    h_in[m, :, place].astype(jnp.float32) + branch
                ).astype(jnp.bfloat16)
                forward_copy(m, part).start()
            start_halos(0, m)

        return carry

    lax.fori_loop(0, micros, forward, 0)

    @pl.when(jnp.logical_not(last))
    def _():
        start_acts()

    def block(i, side):
        start = pl.multiple_of((2 * i + side) * rows, 8)
        return point_sum[pl.ds(start, rows), :]

    def send_pair(i, carry):
        pair_out[i] = block(i, 1 - parity).astype(jnp.bfloat16)
        pair_copy(i).start()
        return carry

    def send_point():
        every = micros * positions
        point_sum[...] = dot_tn(mix[...].reshape(every, inner), e_in[...].reshape(every, channels))
        lax.fori_loop(0, half, send_pair, 0)

    def backward(m, carry):
        @pl.when(last)
        def _():
            e_in[m] = grad_out[m]

        @pl.when(jnp.logical_not(last))
        def _():
            backward_copy(m).wait_recv()

        grad_mix = dot_nt(e_in[m], w_point[...])
        grad_conv, grad_gain = act_pull(conv[m], gain_point[...], grad_mix)
        gains[:, channels:] += grad_gain
        own = grad_conv.astype(jnp.bfloat16)
        q_own[m] = own
        start_halos(1, m)
        each_column_peer(lambda off: q_copy(m, off).start())
        own_pass_copy(m).start()

        @pl.when(jnp.logical_and(first, m == micros - 1))
        def _():
            send_point()

        back = dot_nt(own, w_conv[channels : 2 * channels])
        wait_halos(1, m)
        back = back + dot_nt(later_of(own, halo_q[m, 1]), w_conv[:channels])
        back = back + dot_nt(earlier_of(own, halo_q[m, 0]), w_conv[2 * channels :])
        grad_in, grad_gain = act_pull(h_in[m].astype(jnp.float32), gain_conv[...], back)
        gains[:, :channels] += grad_gain
        grads[m] = (e_in[m].astype(jnp.float32) + grad_in).astype(jnp.bfloat16)

        @pl.when(jnp.logical_not(first))
        def _():
            backward_copy(m).start()

        @pl.when(m > 0)
        def _():
            pass_on(m - 1)

        return carry

    lax.fori_loop(0, micros, backward, 0)

    @pl.when(jnp.logical_not(first))
    def _():
        send_point()

    each_peer(lambda off: gains_copy(off).start())
    pass_on(micros - 1)

    def add_pair(i, carry):
        pair_copy(i).wait_recv()
        point_out[i] = (block(i, parity) + pair_in[i].astype(jnp.float32)).astype(jnp.bfloat16)
        return carry

    lax.fori_loop(0, half, add_pair, 0)
    each_column_peer(lambda off: point_copy(off).start())

    @pl.when(last)
    def _():
        start_acts()

    own_copies = [
        pltpu.make_async_copy(point_out.at[spot], point_all.at[spot], own_sem.at[0]),
        pltpu.make_async_copy(gains, gains_all.at[me], own_sem.at[1]),
    ]
    for m in range(micros):
        own_copies += [
            pltpu.make_async_copy(acts_part(m, me), acts_all.at[me, m], own_sem.at[2 + 2 * m]),
            pltpu.make_async_copy(q_own.at[m], q_all.at[me, m], own_sem.at[3 + 2 * m]),
        ]
    for copy in own_copies:
        copy.start()
    for copy in own_copies:
        copy.wait()

    def finish(m, carry):
        wait_halo_sends(1, m)

        @pl.when(first)
        def _():
            wait_halo_sends(2, m)

        @pl.when(jnp.logical_not(last))
        def _():
            wait_halo_sends(0, m)
            for part in range(2):
                forward_copy(m, part).wait_send()

        @pl.when(jnp.logical_not(first))
        def _():
            backward_copy(m).wait_send()

        each_peer(lambda off: acts_copy(m, off).wait())
        each_column_peer(lambda off: q_copy(m, off).wait_send())
        own_pass_copy(m).wait()
        each_column_peer(lambda off: pass_copy(m, off).wait())
        return carry

    lax.fori_loop(0, micros, finish, 0)
    each_peer(lambda off: gains_copy(off).wait())
    each_column_peer(lambda off: point_copy(off).wait())

    def finish_pair(i, carry):
        pair_copy(i).wait_send()
        return carry

    lax.fori_loop(0, half, finish_pair, 0)


def on_device(inputs, grad_out, w_conv, w_point, gain_conv, gain_point):
    micros, positions, channels = inputs.shape
    sections, group = lax.axis_size("section"), lax.axis_size("dp")
    me = lax.axis_index("dp")
    inner = w_conv.shape[2]
    norm_scale = 1.0 / math.sqrt(micros * positions * group)
    reach = 3 ** (sections - 1) // 2 ** (sections - 1)
    halo = -(-reach // 16) * 16
    share, rows = 3 * channels // group, inner // group
    wide = window(share)
    half = group // 2
    bf16, f32 = jnp.bfloat16, jnp.float32
    dma = pltpu.SemaphoreType.DMA
    vmem = pl.BlockSpec(memory_space=pltpu.VMEM)
    anywhere = pl.BlockSpec(memory_space=pl.ANY)
    with jax.named_scope("tower"):
        grads, acts_all, q_all, point_all, gains_all = pl.pallas_call(
            functools.partial(tower, sections, group, halo),
            out_shape=[
                jax.ShapeDtypeStruct(inputs.shape, bf16),
                jax.ShapeDtypeStruct((group, micros, positions, wide), bf16),
                jax.ShapeDtypeStruct((group, micros, positions, inner), bf16),
                jax.ShapeDtypeStruct((half, rows, channels), bf16),
                jax.ShapeDtypeStruct((group, 1, channels + inner), f32),
            ],
            in_specs=[vmem] * 6,
            out_specs=[vmem] + [anywhere] * 4,
            scratch_shapes=[
                pltpu.VMEM((micros, positions, channels), bf16),
                pltpu.VMEM((micros, positions, channels), bf16),
                pltpu.VMEM((micros, positions, channels), bf16),
                pltpu.VMEM((micros, positions, inner), f32),
                pltpu.VMEM((micros, positions, inner), bf16),
                pltpu.VMEM((micros, positions, 3 * channels), bf16),
                pltpu.VMEM((micros, positions, inner), bf16),
                pltpu.VMEM((micros, 2, halo, channels), bf16),
                pltpu.VMEM((micros, 2, halo, inner), bf16),
                pltpu.VMEM((inner, channels), f32),
                pltpu.VMEM((half, rows, channels), bf16),
                pltpu.VMEM((half, rows, channels), bf16),
                pltpu.VMEM((half, rows, channels), bf16),
                pltpu.VMEM((1, channels + inner), f32),
                dma((3, micros)), dma((3, micros)),
                dma((3, micros, 2)), dma((3, micros, 2)),
                dma((micros, group)), dma((micros, group)),
                dma((micros, half)), dma((micros, half)),
                dma((micros, half)), dma((micros, half)),
                dma((half,)), dma((half,)),
                dma((half,)), dma((half,)),
                dma((group,)), dma((group,)),
                dma((2 + 2 * micros,)),
            ],
            compiler_params=pltpu.CompilerParams(
                collective_id=0, has_side_effects=True, vmem_limit_bytes=56 * 2**20
            ),
        )(inputs, grad_out, w_conv[0], w_point[0], gain_conv, gain_point)

    total = group * micros * positions
    conv_rows = lax.dot_general(
        acts_all.reshape(total, wide), q_all.reshape(total, inner),
        (((0,), (0,)), ((), ())), preferred_element_type=f32,
    )
    share_conv = lax.dynamic_slice_in_dim(conv_rows, lax.rem(share * me, 128), share, 0)
    share_point = jnp.sum(point_all.astype(f32), axis=0)
    gains = jnp.sum(gains_all, axis=(0, 1))
    own_c, own_p = channels // group, inner // group
    share_gc = lax.dynamic_slice_in_dim(gains, me * own_c, own_c, 0)
    share_gp = lax.dynamic_slice_in_dim(gains, channels + me * own_p, own_p, 0)
    return (
        (share_conv * norm_scale)[None],
        (share_point * norm_scale)[None],
        (share_gc * norm_scale)[None],
        (share_gp * norm_scale)[None],
        grads[None],
    )


def solution(mesh):
    return jax.shard_map(
        on_device,
        mesh=mesh,
        in_specs=(
            P(None, "dp", None),
            P(None, "dp", None),
            P("section", None, None),
            P("section", None, None),
            P("section", None),
            P("section", None),
        ),
        out_specs=(
            P("section", "dp", None),
            P("section", "dp", None),
            P("section", "dp"),
            P("section", "dp"),
            P("section", None, "dp", None),
        ),
        check_vma=False,
    )
```

```python
import functools
import math

import jax
import jax.numpy as jnp
from jax import lax
from jax.experimental import pallas as pl
from jax.experimental.pallas import tpu as pltpu
from jax.sharding import PartitionSpec as P

EPSILON = 1e-06
MESH = pl.DeviceIdType.MESH
GELU_C = math.sqrt(2.0 / math.pi)


def normed(values):
    mean_sq = jnp.mean(values * values, axis=-1, keepdims=True)
    rate = lax.rsqrt(mean_sq + EPSILON)
    return values * rate, rate


def gelu(u):
    return 0.5 * u * (1.0 + jnp.tanh(GELU_C * (u + 0.044715 * u * u * u)))


def act_pull(values, gain, upstream):
    unit, rate = normed(values)
    u = unit * gain
    square = u * u
    bent = jnp.tanh(GELU_C * (u + 0.044715 * square * u))
    slope = 0.5 * (1.0 + bent) + 0.5 * u * (1.0 - bent * bent) * GELU_C * (
        1.0 + 3.0 * 0.044715 * square
    )
    inner = upstream * slope
    grad_gain = jnp.sum(inner * unit, axis=0, keepdims=True)
    scaled = inner * gain
    drift = jnp.mean(scaled * unit, axis=-1, keepdims=True)
    return rate * (scaled - unit * drift), grad_gain


def dot(left, right):
    return jnp.dot(left, right, preferred_element_type=jnp.float32)


def dot_nt(left, right):
    return lax.dot_general(
        left, right, (((1,), (1,)), ((), ())), preferred_element_type=jnp.float32
    )


def dot_tn(left, right):
    return lax.dot_general(
        left, right, (((0,), (0,)), ((), ())), preferred_element_type=jnp.float32
    )


def pick(rows, source_rows, offset):
    row = lax.broadcasted_iota(jnp.int32, (rows, source_rows), 0)
    column = lax.broadcasted_iota(jnp.int32, (rows, source_rows), 1)
    return jnp.where(column - row == offset, 1.0, 0.0).astype(jnp.bfloat16)


def window(share):
    most = max((share * j) % 128 for j in range(128))
    return -(-(share + most) // 128) * 128


def tower(
    sections, group, halo,
    inputs, grad_out, w_conv, w_point, gain_conv, gain_point,
    grads, conv_rows, point_all, gains_all,
    acts_all, q_all, h_in, h_out, e_in, conv, mix, columns, q_own, halo_a, halo_q, point_sum, pair_out, pair_in,
    point_out, gains,
    sec_send, sec_recv, halo_send, halo_recv,
    acts_send, acts_recv, q_send, q_recv, pass_send, pass_recv, pair_send, pair_recv,
    point_send, point_recv, gains_send, gains_recv, own_sem,
):
    section = lax.axis_index("section")
    me = lax.axis_index("dp")
    micros, positions, channels = inputs.shape
    inner = w_conv.shape[1]
    share = 3 * channels // group
    wide = window(share)
    first, last = section == 0, section == sections - 1
    left_end, right_end = me == 0, me == group - 1
    half = group // 2
    parity, spot = lax.rem(me, 2), me // 2
    partner = me + 1 - 2 * parity
    rows = inner // group

    dilation = jnp.int32(1)
    for index in range(sections):
        dilation = jnp.where(section == index, 3**index // 2**index, dilation)

    halo_a[...] = jnp.zeros_like(halo_a)
    halo_q[...] = jnp.zeros_like(halo_q)
    gains[...] = jnp.zeros_like(gains)

    barrier = pltpu.get_barrier_semaphore()

    def greet(off, carry):
        pl.semaphore_signal(
            barrier, inc=1, device_id={"dp": lax.rem(me + off, group)}, device_id_type=MESH
        )
        return carry

    lax.fori_loop(1, group, greet, 0)

    @pl.when(jnp.logical_not(first))
    def _():
        pl.semaphore_signal(barrier, inc=1, device_id={"section": section - 1}, device_id_type=MESH)

    @pl.when(jnp.logical_not(last))
    def _():
        pl.semaphore_signal(barrier, inc=1, device_id={"section": section + 1}, device_id_type=MESH)

    def greet_diagonal(there, step, by):
        @pl.when(jnp.logical_and(there, jnp.logical_not(left_end if step < 0 else right_end)))
        def _():
            pl.semaphore_signal(
                barrier, inc=1, device_id={"section": section + by, "dp": me + step},
                device_id_type=MESH,
            )

    for step in (-1, 1):
        greet_diagonal(jnp.logical_not(first), step, -1)
        greet_diagonal(jnp.logical_not(last), step, 1)
    beside = jnp.where(first, 0, 1) + jnp.where(last, 0, 1)
    ends = jnp.where(left_end, 0, 1) + jnp.where(right_end, 0, 1)
    pl.semaphore_wait(barrier, group - 1 + beside * (1 + ends))

    def remote(src, dst, send, recv, device):
        return pltpu.make_async_remote_copy(
            src_ref=src, dst_ref=dst, send_sem=send, recv_sem=recv,
            device_id=device, device_id_type=MESH,
        )

    def forward_copy(m, part):
        place = pl.ds(part * (channels // 2), channels // 2)
        return remote(
            h_out.at[m, :, place], h_in.at[m, :, place],
            sec_send.at[part, m], sec_recv.at[part, m], {"section": section + 1},
        )

    def backward_copy(m):
        return remote(
            grads.at[m], e_in.at[m], sec_send.at[2, m], sec_recv.at[2, m], {"section": section - 1}
        )

    def halo_copy(kind, m, side):
        rows = pl.ds(positions - halo, halo) if side == 0 else pl.ds(0, halo)
        device = {"dp": me + 1 if side == 0 else me - 1}
        if kind == 0:
            src, store = h_out.at[m, rows], halo_a
            device["section"] = section + 1
        elif kind == 1:
            src, store = q_own.at[m, rows], halo_q
        else:
            src, store = inputs.at[m, rows], halo_a
        return remote(
            src, store.at[m, side], halo_send.at[kind, m, side], halo_recv.at[kind % 2, m, side],
            device,
        )

    def start_halos(kind, m):
        @pl.when(jnp.logical_not(right_end))
        def _():
            halo_copy(kind, m, 0).start()

        @pl.when(jnp.logical_not(left_end))
        def _():
            halo_copy(kind, m, 1).start()

    def wait_halos(kind, m):
        @pl.when(jnp.logical_not(left_end))
        def _():
            halo_copy(kind, m, 0).wait_recv()

        @pl.when(jnp.logical_not(right_end))
        def _():
            halo_copy(kind, m, 1).wait_recv()

    def wait_halo_sends(kind, m):
        @pl.when(jnp.logical_not(right_end))
        def _():
            halo_copy(kind, m, 0).wait_send()

        @pl.when(jnp.logical_not(left_end))
        def _():
            halo_copy(kind, m, 1).wait_send()

    def acts_part(m, owner):
        start = pl.multiple_of((share * owner) // 128 * 128, 128)
        return columns.at[m, :, pl.ds(start, wide)]

    def acts_copy(m, off):
        peer = lax.rem(me + off, group)
        return remote(
            acts_part(m, peer), acts_all.at[me, m], acts_send.at[m, off], acts_recv.at[m, off],
            {"dp": peer},
        )

    def column_peer(off):
        return 2 * lax.rem(spot + off, half) + parity

    def q_copy(m, off):
        return remote(
            q_own.at[m], q_all.at[me, m], q_send.at[m, off], q_recv.at[m, off],
            {"dp": column_peer(off)},
        )

    def pass_copy(m, off):
        source = 2 * lax.rem(spot - off + half, half) + parity
        return remote(
            q_all.at[source, m], q_all.at[source, m], pass_send.at[m, off], pass_recv.at[m, off],
            {"dp": partner},
        )

    def own_pass_copy(m):
        return remote(
            q_own.at[m], q_all.at[me, m], pass_send.at[m, 0], pass_recv.at[m, 0],
            {"dp": partner},
        )

    def pair_copy(i):
        return remote(
            pair_out.at[i], pair_in.at[i], pair_send.at[i], pair_recv.at[i], {"dp": partner}
        )

    def point_copy(off):
        return remote(
            point_out.at[lax.rem(spot + off, half)], point_all.at[spot],
            point_send.at[off], point_recv.at[off], {"dp": column_peer(off)},
        )

    def gains_copy(off):
        peer = lax.rem(me + off, group)
        return remote(
            gains, gains_all.at[me], gains_send.at[off], gains_recv.at[off], {"dp": peer}
        )

    def each_peer(action):
        def step(off, carry):
            action(off)
            return carry

        lax.fori_loop(1, group, step, 0)

    def each_column_peer(action):
        def step(off, carry):
            action(off)
            return carry

        lax.fori_loop(1, half, step, 0)

    def pass_on(m):
        def step(off):
            q_copy(m, off).wait_recv()
            pass_copy(m, off).start()

        each_column_peer(step)

    def start_acts():
        def step(m, carry):
            each_peer(lambda off: acts_copy(m, off).start())
            return carry

        lax.fori_loop(0, micros, step, 0)

    def earlier_of(own, store):
        return (
            dot(pick(positions, positions, -dilation), own)
            + dot(pick(positions, halo, halo - dilation), store)
        ).astype(jnp.bfloat16)

    def later_of(own, store):
        return (
            dot(pick(positions, positions, dilation), own)
            + dot(pick(positions, halo, dilation - positions), store)
        ).astype(jnp.bfloat16)

    @pl.when(first)
    def _():
        for m in range(micros):
            start_halos(2, m)

    def forward(m, carry):
        @pl.when(first)
        def _():
            h_in[m] = inputs[m]

        @pl.when(jnp.logical_not(first))
        def _():
            for part in range(2):
                forward_copy(m, part).wait_recv()

        def activated(values):
            unit, _unused = normed(values.astype(jnp.float32))
            return gelu(unit * gain_conv[...]).astype(jnp.bfloat16)

        own = activated(h_in[m])
        columns[m, :, channels : 2 * channels] = own
        total = dot(own, w_conv[channels : 2 * channels])
        wait_halos(0, m)
        earlier = earlier_of(own, activated(halo_a[m, 0]))
        columns[m, :, :channels] = earlier
        total = total + dot(earlier, w_conv[:channels])
        later = later_of(own, activated(halo_a[m, 1]))
        columns[m, :, 2 * channels :] = later
        total = total + dot(later, w_conv[2 * channels :])
        conv[m] = total
        unit, _unused = normed(total)
        mixture = gelu(unit * gain_point[...]).astype(jnp.bfloat16)
        mix[m] = mixture

        @pl.when(jnp.logical_not(last))
        def _():
            for part in range(2):
                place = slice(part * (channels // 2), (part + 1) * (channels // 2))
                branch = dot(mix[m], w_point[:, place])
                h_out[m, :, place] = (
                    h_in[m, :, place].astype(jnp.float32) + branch
                ).astype(jnp.bfloat16)
                forward_copy(m, part).start()
            start_halos(0, m)

        return carry

    lax.fori_loop(0, micros, forward, 0)

    early = section < sections // 2

    @pl.when(early)
    def _():
        start_acts()

    def block(i, side):
        start = pl.multiple_of((2 * i + side) * rows, 8)
        return point_sum[pl.ds(start, rows), :]

    def send_pair(i, carry):
        pair_out[i] = block(i, 1 - parity).astype(jnp.bfloat16)
        pair_copy(i).start()
        return carry

    def send_point():
        every = micros * positions
        point_sum[...] = dot_tn(mix[...].reshape(every, inner), e_in[...].reshape(every, channels))
        lax.fori_loop(0, half, send_pair, 0)

    def backward(m, carry):
        @pl.when(last)
        def _():
            e_in[m] = grad_out[m]

        @pl.when(jnp.logical_not(last))
        def _():
            backward_copy(m).wait_recv()

        grad_mix = dot_nt(e_in[m], w_point[...])
        grad_conv, grad_gain = act_pull(conv[m], gain_point[...], grad_mix)
        gains[:, channels:] += grad_gain
        own = grad_conv.astype(jnp.bfloat16)
        q_own[m] = own
        start_halos(1, m)
        each_column_peer(lambda off: q_copy(m, off).start())
        own_pass_copy(m).start()

        @pl.when(jnp.logical_and(first, m == micros - 1))
        def _():
            send_point()

        back = dot_nt(own, w_conv[channels : 2 * channels])
        wait_halos(1, m)
        back = back + dot_nt(later_of(own, halo_q[m, 1]), w_conv[:channels])
        back = back + dot_nt(earlier_of(own, halo_q[m, 0]), w_conv[2 * channels :])
        grad_in, grad_gain = act_pull(h_in[m].astype(jnp.float32), gain_conv[...], back)
        gains[:, :channels] += grad_gain
        grads[m] = (e_in[m].astype(jnp.float32) + grad_in).astype(jnp.bfloat16)

        @pl.when(jnp.logical_not(first))
        def _():
            backward_copy(m).start()

        @pl.when(m > 0)
        def _():
            pass_on(m - 1)

        return carry

    lax.fori_loop(0, micros, backward, 0)

    @pl.when(jnp.logical_not(first))
    def _():
        send_point()

    each_peer(lambda off: gains_copy(off).start())
    pass_on(micros - 1)

    def add_pair(i, carry):
        pair_copy(i).wait_recv()
        point_out[i] = (block(i, parity) + pair_in[i].astype(jnp.float32)).astype(jnp.bfloat16)
        return carry

    lax.fori_loop(0, half, add_pair, 0)
    each_column_peer(lambda off: point_copy(off).start())

    @pl.when(jnp.logical_not(early))
    def _():
        start_acts()

    own_copies = [
        pltpu.make_async_copy(point_out.at[spot], point_all.at[spot], own_sem.at[0]),
        pltpu.make_async_copy(gains, gains_all.at[me], own_sem.at[1]),
    ]
    for m in range(micros):
        own_copies += [
            pltpu.make_async_copy(acts_part(m, me), acts_all.at[me, m], own_sem.at[2 + 2 * m]),
            pltpu.make_async_copy(q_own.at[m], q_all.at[me, m], own_sem.at[3 + 2 * m]),
        ]
    for copy in own_copies:
        copy.start()
    for copy in own_copies:
        copy.wait()

    conv_rows[...] = jnp.zeros_like(conv_rows)

    def finish(m, carry):
        wait_halo_sends(1, m)

        @pl.when(first)
        def _():
            wait_halo_sends(2, m)

        @pl.when(jnp.logical_not(last))
        def _():
            wait_halo_sends(0, m)
            for part in range(2):
                forward_copy(m, part).wait_send()

        @pl.when(jnp.logical_not(first))
        def _():
            backward_copy(m).wait_send()

        each_peer(lambda off: acts_copy(m, off).wait())
        each_column_peer(lambda off: q_copy(m, off).wait_send())
        own_pass_copy(m).wait()
        each_column_peer(lambda off: pass_copy(m, off).wait())

        def contract(pair, inner_carry):
            both = pl.ds(2 * pair, 2)
            left = acts_all[both, m].reshape(2 * positions, wide)
            right = q_all[both, m].reshape(2 * positions, inner)
            conv_rows[...] += dot_tn(left, right)
            return inner_carry

        lax.fori_loop(0, half, contract, 0)
        return carry

    lax.fori_loop(0, micros, finish, 0)
    each_peer(lambda off: gains_copy(off).wait())
    each_column_peer(lambda off: point_copy(off).wait())

    def finish_pair(i, carry):
        pair_copy(i).wait_send()
        return carry

    lax.fori_loop(0, half, finish_pair, 0)


def on_device(inputs, grad_out, w_conv, w_point, gain_conv, gain_point):
    micros, positions, channels = inputs.shape
    sections, group = lax.axis_size("section"), lax.axis_size("dp")
    me = lax.axis_index("dp")
    inner = w_conv.shape[2]
    norm_scale = 1.0 / math.sqrt(micros * positions * group)
    reach = 3 ** (sections - 1) // 2 ** (sections - 1)
    halo = -(-reach // 16) * 16
    share, rows = 3 * channels // group, inner // group
    wide = window(share)
    half = group // 2
    bf16, f32 = jnp.bfloat16, jnp.float32
    dma = pltpu.SemaphoreType.DMA
    vmem = pl.BlockSpec(memory_space=pltpu.VMEM)
    anywhere = pl.BlockSpec(memory_space=pl.ANY)
    with jax.named_scope("tower"):
        grads, conv_rows, point_all, gains_all = pl.pallas_call(
            functools.partial(tower, sections, group, halo),
            out_shape=[
                jax.ShapeDtypeStruct(inputs.shape, bf16),
                jax.ShapeDtypeStruct((wide, inner), f32),
                jax.ShapeDtypeStruct((half, rows, channels), bf16),
                jax.ShapeDtypeStruct((group, 1, channels + inner), f32),
            ],
            in_specs=[vmem] * 6,
            out_specs=[vmem] * 2 + [anywhere] * 2,
            scratch_shapes=[
                pltpu.VMEM((group, micros, positions, wide), bf16),
                pltpu.VMEM((group, micros, positions, inner), bf16),
                pltpu.VMEM((micros, positions, channels), bf16),
                pltpu.VMEM((micros, positions, channels), bf16),
                pltpu.VMEM((micros, positions, channels), bf16),
                pltpu.VMEM((micros, positions, inner), f32),
                pltpu.VMEM((micros, positions, inner), bf16),
                pltpu.VMEM((micros, positions, 3 * channels), bf16),
                pltpu.VMEM((micros, positions, inner), bf16),
                pltpu.VMEM((micros, 2, halo, channels), bf16),
                pltpu.VMEM((micros, 2, halo, inner), bf16),
                pltpu.VMEM((inner, channels), f32),
                pltpu.VMEM((half, rows, channels), bf16),
                pltpu.VMEM((half, rows, channels), bf16),
                pltpu.VMEM((half, rows, channels), bf16),
                pltpu.VMEM((1, channels + inner), f32),
                dma((3, micros)), dma((3, micros)),
                dma((3, micros, 2)), dma((3, micros, 2)),
                dma((micros, group)), dma((micros, group)),
                dma((micros, half)), dma((micros, half)),
                dma((micros, half)), dma((micros, half)),
                dma((half,)), dma((half,)),
                dma((half,)), dma((half,)),
                dma((group,)), dma((group,)),
                dma((2 + 2 * micros,)),
            ],
            compiler_params=pltpu.CompilerParams(
                collective_id=0, has_side_effects=True, vmem_limit_bytes=56 * 2**20
            ),
        )(inputs, grad_out, w_conv[0], w_point[0], gain_conv, gain_point)

    share_conv = lax.dynamic_slice_in_dim(conv_rows, lax.rem(share * me, 128), share, 0)
    share_point = jnp.sum(point_all.astype(f32), axis=0)
    gains = jnp.sum(gains_all, axis=(0, 1))
    own_c, own_p = channels // group, inner // group
    share_gc = lax.dynamic_slice_in_dim(gains, me * own_c, own_c, 0)
    share_gp = lax.dynamic_slice_in_dim(gains, channels + me * own_p, own_p, 0)
    return (
        (share_conv * norm_scale)[None],
        (share_point * norm_scale)[None],
        (share_gc * norm_scale)[None],
        (share_gp * norm_scale)[None],
        grads[None],
    )


def solution(mesh):
    return jax.shard_map(
        on_device,
        mesh=mesh,
        in_specs=(
            P(None, "dp", None),
            P(None, "dp", None),
            P("section", None, None),
            P("section", None, None),
            P("section", None),
            P("section", None),
        ),
        out_specs=(
            P("section", "dp", None),
            P("section", "dp", None),
            P("section", "dp"),
            P("section", "dp"),
            P("section", None, "dp", None),
        ),
        check_vma=False,
    )
```
